256 devices in a mesh: leaf: 32 (over z_lo, y, core), top: 8 (over x, z_hi).
Axes of the slice: x: 4, y: 4, z: 8 (z_hi: 2, z_lo: 4; z = z_hi * 4 + z_lo), core: 2. Of those that a mesh axis runs over, the one named last changes fastest.
Arguments:
- vectors: bfloat16 [8, 32, 768, 512], P('top', 'leaf'), may hold values from -6 to 6
- near_tiles: bfloat16 [8, 32, 8, 768, 768], P('top', 'leaf'), may hold values from -0.078125 to 0.078125
- leaf_basis: bfloat16 [8, 32, 768, 128], P('top', 'leaf'), may hold values from -0.21875 to 0.21875
- transfer: bfloat16 [8, 32, 128, 128], P('top', 'leaf'), may hold values from -0.25 to 0.25
- coupling: bfloat16 [8, 32, 7, 128, 128], P('top', 'leaf'), may hold values from -0.1875 to 0.1875
- top_coupling: bfloat16 [8, 8, 128, 128], P('top'), may hold values from -0.1875 to 0.1875
- near_list: int32 [8, 32, 8], P('top', 'leaf'), may hold values from -4 to 4, as said below
- far_list: int32 [8, 32, 7], P('top', 'leaf'), may hold values from 0 to 31, as said below
- row_counts: int32 [8, 32], P('top', 'leaf'), may hold values from 384 to 768
Outputs:
- product: float32 [8, 32, 768, 512], P('top', 'leaf')
The draws below stay inside these ranges and needn't reach their ends.
Inputs may be any that keep to these rules, and one draw needn't show every extreme that they name: `near_list`: each leaf's 8 offsets are distinct; an offset that leads outside the cluster's 32 leaves stands for an absent block. `far_list`: each leaf's entries are distinct positions in its cluster, each more than 4 away from the leaf's own position. `row_counts`: rows at and beyond the count are padding.
All inputs are finite; a program needn't handle non-finite values.
Results may differ from the reference program's by a relative error of at most 0.0045.
Values may be sent and summed in bfloat16 or wider, within the bound.
No kernel may reach another device: no remote copies, remote signals or barrier semaphores. Data moves between devices by JAX's collectives and lax.ppermute only.
A program may use at most 128 MiB of HBM per device.

```python
import jax
import jax.numpy as jnp
from jax import lax

LEAF_ROWS = 768
RANK = 128
VECS = 512
REACH = 4
NEAR = 8
FAR = 7
CLUSTERS = 8
GROUP = 32
TOPFAR = 8


def draw_near_list(key, part):
    subkeys = jax.random.split(key, CLUSTERS * GROUP)
    orders = jax.vmap(lambda single: jax.random.permutation(single, 2 * REACH + 1))(subkeys)
    return (orders[:, :NEAR] - REACH).astype(jnp.int32).reshape(CLUSTERS, GROUP, NEAR)


def draw_far_list(key, part):
    scores = jax.random.randint(jax.random.fold_in(key, 7), (CLUSTERS, GROUP, GROUP), 0, 1 << 20)
    column = jnp.arange(GROUP, dtype=jnp.int32)
    scores = scores * GROUP + column[None, None, :]
    distance = jnp.abs(column[:, None] - column[None, :])
    scores = jnp.where(distance[None] > REACH, scores, -1)
    values, picked = lax.top_k(scores, FAR)
    return picked.astype(jnp.int32)


def touch_ends(result, stream_key, smallest, high):
    index_at = [jax.random.randint(jax.random.fold_in(stream_key, axis), (), 0, length) for axis, length in enumerate(result.shape)]
    widest = result.shape.index(max(result.shape))
    beside = index_at[:widest] + [(index_at[widest] + 1) % result.shape[widest]] + index_at[widest + 1:]
    return result.at[tuple(index_at)].set(smallest).at[tuple(beside)].set(high)


def shard_levels(own_key, extent, shards, smallest, high):
    gain, own = 1.0, jax.random.fold_in(own_key, 6)
    for dim, blocks in shards:
        heights = jnp.exp(jax.random.uniform(jax.random.fold_in(own, dim), (blocks,), jnp.float32, smallest / len(shards), high / len(shards)))
        gain = gain * jnp.repeat(heights, extent[dim] // blocks).reshape([-1 if axis == dim else 1 for axis in range(len(extent))])
    return gain


def normal_values(stream_key, extent, width, most, cuts=(), kind=jnp.bfloat16):
    factor_of = shard_levels(stream_key, extent, cuts, -0.22, 0.18) if cuts else 1.0
    result = jax.random.normal(stream_key, extent, jnp.float32) * width * factor_of
    return jnp.minimum(jnp.maximum(result, -most), most).astype(kind)


def setup_inputs(seed: int = 0) -> dict:
    streams_of = jax.random.split(jax.random.key(seed), 10)
    vectors = normal_values(streams_of[0], (CLUSTERS, GROUP, LEAF_ROWS, VECS), 1.0, 6.0, ((0, 8), (1, 32)))
    near_tiles = normal_values(streams_of[1], (CLUSTERS, GROUP, NEAR, LEAF_ROWS, LEAF_ROWS), (NEAR * LEAF_ROWS) ** -0.5, 0.078125, ((0, 8), (1, 32)))
    leaf_basis = normal_values(streams_of[2], (CLUSTERS, GROUP, LEAF_ROWS, RANK), LEAF_ROWS ** -0.5, 0.21875, ((0, 8), (1, 32)))
    transfer = normal_values(streams_of[3], (CLUSTERS, GROUP, RANK, RANK), (RANK * 4) ** -0.5, 0.25, ((0, 8), (1, 32)))
    coupling = normal_values(streams_of[4], (CLUSTERS, GROUP, FAR, RANK, RANK), (RANK * FAR) ** -0.5, 0.1875, ((0, 8), (1, 32)))
    top_coupling = normal_values(streams_of[5], (CLUSTERS, TOPFAR, RANK, RANK), (RANK * TOPFAR) ** -0.5, 0.1875, ((0, 8),))
    near_list = draw_near_list(jax.random.fold_in(streams_of[9], 71), 0)
    far_list = draw_far_list(jax.random.fold_in(streams_of[9], 71), 0)
    row_counts = touch_ends(jax.random.randint(streams_of[8], (CLUSTERS, GROUP), LEAF_ROWS // 2, LEAF_ROWS + 1), jax.random.fold_in(streams_of[8], 1), LEAF_ROWS // 2, LEAF_ROWS).astype(jnp.int32)
    return {"vectors": vectors, "near_tiles": near_tiles, "leaf_basis": leaf_basis, "transfer": transfer, "coupling": coupling, "top_coupling": top_coupling, "near_list": near_list, "far_list": far_list, "row_counts": row_counts}


def reference(vectors, near_tiles, leaf_basis, transfer, coupling, top_coupling, near_list, far_list, row_counts):
    row_index = jnp.arange(LEAF_ROWS, dtype=jnp.int32)
    keep = (row_index[None, None, :] < row_counts[:, :, None]).astype(jnp.bfloat16)
    masked = vectors * keep[..., None]

    def near_leaf(index):
        cluster = index // GROUP
        member = index % GROUP
        targets = member + near_list[cluster, member]
        valid = ((targets >= 0) & (targets < GROUP)).astype(jnp.bfloat16)
        safe = jnp.clip(targets, 0, GROUP - 1).astype(jnp.int32)
        sources = masked[cluster][safe] * valid[:, None, None]
        return jnp.einsum("kij,kjv->iv", near_tiles[cluster, member].astype(jnp.float32), sources.astype(jnp.float32))

    near = lax.map(near_leaf, jnp.arange(CLUSTERS * GROUP, dtype=jnp.int32))
    near = near.reshape(CLUSTERS, GROUP, LEAF_ROWS, VECS)

    basis = leaf_basis.astype(jnp.float32)
    nested = transfer.astype(jnp.float32)
    coeff = jnp.einsum("cgir,cgiv->cgrv", basis, masked.astype(jnp.float32)).astype(jnp.bfloat16)
    upward = jnp.einsum("cgab,cgav->cgbv", nested, coeff.astype(jnp.float32))
    parent = jnp.sum(upward, axis=1).astype(jnp.bfloat16)
    cluster_ids = jnp.arange(CLUSTERS, dtype=jnp.int32)
    sibling_ids = (cluster_ids[:, None] + 1 + jnp.arange(TOPFAR, dtype=jnp.int32)[None, :]) % CLUSTERS
    chosen = parent[sibling_ids]
    parent_field = jnp.einsum("cmab,cmbv->cav", top_coupling.astype(jnp.float32), chosen.astype(jnp.float32)).astype(jnp.bfloat16)
    cluster_index = cluster_ids[:, None, None]
    siblings = coeff[cluster_index, far_list]
    local_field = jnp.einsum("cgmab,cgmbv->cgav", coupling.astype(jnp.float32), siblings.astype(jnp.float32))
    local_field = local_field + jnp.einsum("cgab,cbv->cgav", nested, parent_field.astype(jnp.float32))
    local_field = local_field.astype(jnp.bfloat16)
    far = jnp.einsum("cgir,cgrv->cgiv", basis, local_field.astype(jnp.float32))
    return (near + far) * keep[..., None].astype(jnp.float32)
```

```python
import functools

import jax
import jax.numpy as jnp
from jax import lax
from jax.experimental import pallas as pl
from jax.experimental.pallas import tpu as pltpu
from jax.sharding import PartitionSpec as P

Z, Y, CORES = 4, 4, 2
ROW = Y * CORES
CHIPS = Z * Y
F32, BF16 = jnp.float32, jnp.bfloat16
LIMIT = 48 * 1024 * 1024


def chip_step(distance):
    return [
        (p * 2 + c, (p + distance) * 2 + c)
        for p in range(CHIPS)
        for c in range(2)
        if 0 <= p + distance < CHIPS
    ]


def turn(dz, dy):
    return [
        (z * ROW + y * 2 + c, ((z + dz) % Z) * ROW + ((y + dy) % Y) * 2 + c)
        for z in range(Z)
        for y in range(Y)
        for c in range(2)
    ]


SWAP = [(i, i ^ 1) for i in range(2 * CHIPS)]
TO_FIRST = [(2 * p + 1, 2 * p) for p in range(CHIPS)]
TO_SECOND = [(2 * p, 2 * p + 1) for p in range(CHIPS)]


def send(block, route):
    return lax.ppermute(block, "leaf", route)


def dot(a, b, dims=((1,), (0,))):
    return lax.dot_general(a, b, (dims, ((), ())), preferred_element_type=F32)


def cost(flops, moved):
    return pl.CostEstimate(flops=int(flops), bytes_accessed=int(moved), transcendentals=0)


VMEM = pl.BlockSpec(memory_space=pltpu.VMEM)
SMEM = pl.BlockSpec(memory_space=pltpu.SMEM)


def upward_kernel(count_ref, vec_ref, basis_ref, transfer_ref, masked_ref, coeff_ref, up_ref):
    rows = lax.broadcasted_iota(jnp.int32, vec_ref.shape, 0)
    masked = jnp.where(rows < count_ref[0], vec_ref[...].astype(F32), 0.0).astype(BF16)
    masked_ref[...] = masked
    coeff = dot(basis_ref[...], masked, ((0,), (0,))).astype(BF16)
    coeff_ref[...] = coeff
    up_ref[...] = dot(coeff, transfer_ref[...], ((0,), (0,))).astype(BF16)


def upward(count, vec, basis, transfer):
    rows, vecs = vec.shape
    rank = basis.shape[1]
    return pl.pallas_call(
        upward_kernel,
        out_shape=[
            jax.ShapeDtypeStruct((rows, vecs), BF16),
            jax.ShapeDtypeStruct((rank, vecs), BF16),
            jax.ShapeDtypeStruct((vecs, rank), BF16),
        ],
        in_specs=[SMEM, VMEM, VMEM, VMEM],
        out_specs=[VMEM] * 3,
        compiler_params=pltpu.CompilerParams(vmem_limit_bytes=LIMIT),
        cost_estimate=cost(2 * rows * rank * vecs, 2 * rows * vecs * 2),
    )(count, vec, basis, transfer)


def partial_kernel(rank, pick_ref, *refs):
    couplings, coeffs, outs, acc = refs[:Z], refs[Z : Z + ROW], refs[Z + ROW : -1], refs[-1]
    for d in range(Z):
        acc[...] = jnp.zeros_like(acc)
        for s in range(ROW):
            which = pick_ref[d * ROW + s]

            @pl.when(which >= 0)
            def add():
                start = pl.multiple_of(which * rank, rank)
                acc[...] += dot(couplings[d][pl.ds(start, rank), :], coeffs[s][...])

        outs[d][...] = acc[...].astype(outs[d].dtype)


def far_partials(pick, couplings, coeffs):
    rank, vecs = coeffs[0].shape
    return pl.pallas_call(
        functools.partial(partial_kernel, rank),
        out_shape=[jax.ShapeDtypeStruct((rank, vecs), F32 if d == 0 else BF16) for d in range(Z)],
        in_specs=[SMEM] + [VMEM] * (Z + ROW),
        out_specs=[VMEM] * Z,
        scratch_shapes=[pltpu.VMEM((rank, vecs), F32)],
        compiler_params=pltpu.CompilerParams(vmem_limit_bytes=LIMIT),
        cost_estimate=cost(2 * 16 * rank * rank * vecs, 12 * rank * vecs * 2),
    )(pick, *couplings, *coeffs)


def top_kernel(shift_ref, parents_ref, coupling_ref, out_ref):
    total = jnp.zeros(out_ref.shape, F32)
    for c in range(parents_ref.shape[0]):
        total += dot(parents_ref[c], coupling_ref[shift_ref[c]], ((1,), (1,)))
    out_ref[...] = total.astype(BF16)


def top_field(shift, parents, coupling):
    return pl.pallas_call(
        top_kernel,
        out_shape=jax.ShapeDtypeStruct(parents.shape[1:], BF16),
        in_specs=[SMEM, VMEM, VMEM],
        out_specs=VMEM,
        compiler_params=pltpu.CompilerParams(vmem_limit_bytes=LIMIT),
        cost_estimate=cost(2 * 8 * 16 * 128 * 128, 8 * 128 * 128 * 2),
    )(shift, parents, coupling)


def near_first_kernel(count, pick_ref, tile_ref, *refs):
    sources, out_ref = refs[:count], refs[count]
    step = pl.program_id(0)

    @pl.when(step == 0)
    def clear():
        out_ref[...] = jnp.zeros_like(out_ref)

    for s in range(count):

        @pl.when((step == s) & (pick_ref[s] >= 0))
        def add():
            out_ref[...] += dot(tile_ref[0], sources[s][...])


def whole(shape):
    return pl.BlockSpec(shape, lambda i, pick: (0,) * len(shape))


def tile_spec(tiles):
    _, rows, cols = tiles.shape
    return pl.BlockSpec((1, rows, cols), lambda i, pick: (jnp.maximum(pick[i], 0), 0, 0))


def near_first(pick, tiles, sources):
    count = len(sources)
    rows, vecs = sources[0].shape
    return pl.pallas_call(
        functools.partial(near_first_kernel, count),
        out_shape=jax.ShapeDtypeStruct((rows, vecs), F32),
        grid_spec=pltpu.PrefetchScalarGridSpec(
            num_scalar_prefetch=1,
            grid=(count,),
            in_specs=[tile_spec(tiles)] + [whole(s.shape) for s in sources],
            out_specs=whole((rows, vecs)),
        ),
        compiler_params=pltpu.CompilerParams(vmem_limit_bytes=LIMIT),
        cost_estimate=cost(2 * count * rows * rows * vecs, count * rows * (rows + vecs) * 2),
    )(pick, tiles, *sources)


def near_last_kernel(count, pick_ref, tile_ref, *refs):
    sources = refs[:count]
    near_ref, basis_ref, transfer_ref, field_ref, own_ref, a_ref, b_ref, c_ref, out_ref = refs[count:]
    step = pl.program_id(0)

    @pl.when(step == 0)
    def far():
        local = own_ref[...] + a_ref[...].astype(F32) + b_ref[...].astype(F32)
        local += c_ref[...].astype(F32) + dot(transfer_ref[...], field_ref[...], ((1,), (1,)))
        out_ref[...] = near_ref[...] + dot(basis_ref[...], local.astype(BF16))

    for s in range(count):

        @pl.when((step == s) & (pick_ref[s] >= 0))
        def add():
            out_ref[...] += dot(tile_ref[0], sources[s][...])

    @pl.when(step == count - 1)
    def cut():
        rows = lax.broadcasted_iota(jnp.int32, out_ref.shape, 0)
        out_ref[...] = jnp.where(rows < pick_ref[count], out_ref[...], 0.0)


def near_last(pick, tiles, sources, rest):
    count = len(sources)
    rows, vecs = sources[0].shape
    return pl.pallas_call(
        functools.partial(near_last_kernel, count),
        out_shape=jax.ShapeDtypeStruct((rows, vecs), F32),
        grid_spec=pltpu.PrefetchScalarGridSpec(
            num_scalar_prefetch=1,
            grid=(count,),
            in_specs=[tile_spec(tiles)] + [whole(s.shape) for s in (*sources, *rest)],
            out_specs=whole((rows, vecs)),
        ),
        compiler_params=pltpu.CompilerParams(vmem_limit_bytes=LIMIT),
        cost_estimate=cost(2 * count * rows * rows * vecs, count * rows * (rows + vecs) * 2),
    )(pick, tiles, *sources, *rest)


def index_of(wanted, entries):
    places = jnp.arange(entries.shape[-1], dtype=jnp.int32)
    return jnp.max(jnp.where(entries == wanted[..., None], places, -1), axis=-1).astype(jnp.int32)


def body(
    vectors,
    near_tiles,
    leaf_basis,
    transfer,
    coupling,
    top_coupling,
    near_list,
    far_list,
    row_counts,
):
    me = lax.axis_index("leaf").astype(jnp.int32)
    mine = lax.axis_index("top").astype(jnp.int32)
    clusters = lax.axis_size("top")
    leaves = lax.axis_size("leaf")
    core, chip_y, row = me % 2, (me // 2) % Y, me // ROW
    basis, nested, tiles = leaf_basis[0, 0], transfer[0, 0], near_tiles[0, 0]
    far_count, rank, _ = coupling.shape[2:]
    vecs = vectors.shape[3]
    count = row_counts[0]

    masked, coeff, up = upward(count, vectors[0, 0], basis, nested)

    from_low = send(masked, chip_step(1))
    from_high = send(masked, chip_step(-1))
    beside = send(masked, SWAP)

    listed = jnp.zeros((16, rank), BF16).at[0, :far_count].set(far_list[0, 0].astype(BF16))
    packet = jnp.concatenate([coupling[0, 0].reshape(far_count * rank, rank), listed])
    packets = [packet] + [send(packet, turn(d, 0)) for d in range(1, Z)]

    across = [coeff] + [send(coeff, turn(0, d)) for d in range(1, Y)]
    coeffs = across + [send(block, SWAP) for block in across]
    steps = jnp.arange(Y, dtype=jnp.int32)
    seats = ((chip_y - steps) % Y) * 2 + row * ROW
    owners = jnp.concatenate([seats + core, seats + 1 - core])
    lists = jnp.stack([p[far_count * rank, :far_count] for p in packets]).astype(jnp.int32)
    lists = lists.at[0].set(far_list[0, 0])
    far_pick = index_of(jnp.broadcast_to(owners[None], (Z, ROW)), lists[:, None, :])

    pieces = lax.all_to_all(up, "leaf", 0, 0, tiled=True).reshape(leaves, vecs // leaves, rank)
    parent = jnp.sum(pieces.astype(F32), axis=0).astype(BF16)
    parents = lax.all_to_all(
        jnp.broadcast_to(parent[None], (clusters, *parent.shape)), "top", 0, 0, tiled=True
    )
    shift = (jnp.arange(clusters, dtype=jnp.int32) + 2 * clusters - 1 - mine) % clusters
    piece = top_field(shift, parents, top_coupling[0])
    field = lax.all_to_all(
        jnp.broadcast_to(piece[None], (leaves, *piece.shape)), "leaf", 0, 0, tiled=True
    ).reshape(vecs, rank)

    own, *others = far_partials(far_pick.reshape(-1), packets, coeffs)
    back = [send(block, turn(-d, 0)) for d, block in zip(range(1, Z), others, strict=True)]

    from_low2 = send(from_low, chip_step(1))
    from_high2 = send(from_high, chip_step(-1))
    low_beside = send(from_low, SWAP)
    high_beside = send(from_high, SWAP)
    side = 1 - 2 * core
    zero = jnp.int32(0)
    first_at = jnp.stack([zero, side, zero - 2, zero + 2, side - 2, side + 2])
    absent = jnp.int32(99)
    last_at = jnp.stack(
        [zero - 4, zero + 4, jnp.where(core == 0, -3, absent), jnp.where(core == 1, 3, absent)]
    )
    offsets = near_list[0, 0][None]
    near = near_first(
        index_of(first_at, offsets),
        tiles,
        [masked, beside, from_low, from_high, low_beside, high_beside],
    )
    low2_beside = send(from_low2, TO_FIRST)
    high2_beside = send(from_high2, TO_SECOND)
    result = near_last(
        jnp.concatenate([index_of(last_at, offsets), count]),
        tiles,
        [from_low2, from_high2, low2_beside, high2_beside],
        [near, basis, nested, field, own, *back],
    )
    return result[None, None]


def solution(mesh):
    in_specs = (
        P("top", "leaf", None, None),
        P("top", "leaf", None, None, None),
        P("top", "leaf", None, None),
        P("top", "leaf", None, None),
        P("top", "leaf", None, None, None),
        P("top", None, None, None),
        P("top", "leaf", None),
        P("top", "leaf", None),
        P("top", "leaf"),
    )
    out_specs = P("top", "leaf", None, None)
    return jax.shard_map(body, mesh=mesh, in_specs=in_specs, out_specs=out_specs, check_vma=False)
```

```python
import jax
import jax.numpy as jnp
from jax import lax
from jax.experimental import pallas as pl
from jax.experimental.pallas import tpu as pltpu
from jax.sharding import PartitionSpec as P

Z, Y, CORES = 4, 4, 2
ROW = Y * CORES
CHIPS = Z * Y
X, HALVES = 4, 2
F32, BF16 = jnp.float32, jnp.bfloat16
LIMIT, FULL = 40 * 1024 * 1024, 60 * 1024 * 1024


def chip_step(distance):
    return [
        (p * 2 + c, (p + distance) * 2 + c)
        for p in range(CHIPS)
        for c in range(2)
        if 0 <= p + distance < CHIPS
    ]


def seat_of(z, y, c):
    return z * ROW + y * 2 + c


def turn(dz, dy):
    return [
        (seat_of(z, y, c), seat_of((z + dz) % Z, (y + dy) % Y, c))
        for z in range(Z)
        for y in range(Y)
        for c in range(2)
    ]


SWAP = [(i, i ^ 1) for i in range(2 * CHIPS)]
TO_FIRST = [(2 * p + 1, 2 * p) for p in range(CHIPS)]
TO_SECOND = [(2 * p, 2 * p + 1) for p in range(CHIPS)]


def send(name, block, route, axis="leaf"):
    with jax.named_scope(name):
        return lax.ppermute(block, axis, route)


def exchange(name, blocks, groups, axis="leaf"):
    with jax.named_scope(name):
        return lax.all_to_all(blocks, axis, 0, 0, tiled=True, axis_index_groups=groups)


def after(blocks, other):
    return lax.optimization_barrier([*blocks, other])[:-1]


def dot(a, b, dims=((1,), (0,))):
    return lax.dot_general(a, b, (dims, ((), ())), preferred_element_type=F32)


def cost(flops, moved):
    return pl.CostEstimate(flops=int(flops), bytes_accessed=int(moved), transcendentals=0)


ANY = pl.BlockSpec(memory_space=pl.ANY)
SMEM = pl.BlockSpec(memory_space=pltpu.SMEM)


def shape(dims, dtype=BF16):
    return jax.ShapeDtypeStruct(dims, dtype)


def call(kernel, scalars, arrays, outs, scratch, copies, price, limit=LIMIT):
    return pl.pallas_call(
        kernel,
        out_shape=outs,
        in_specs=[SMEM] * len(scalars) + [ANY] * len(arrays),
        out_specs=[ANY] * len(outs),
        scratch_shapes=[*scratch, pltpu.SemaphoreType.DMA((copies,))],
        compiler_params=pltpu.CompilerParams(vmem_limit_bytes=limit),
        cost_estimate=price,
    )(*scalars, *arrays)


class Mover:
    def __init__(self, sems):
        self.sems, self.used = sems, 0

    def __call__(self, src, dst):
        copy = pltpu.make_async_copy(src, dst, self.sems.at[self.used])
        self.used += 1
        copy.start()
        return copy

    def later(self, src, dst):
        copy = pltpu.make_async_copy(src, dst, self.sems.at[self.used])
        self.used += 1
        return copy


def coeff_kernel(count_ref, vec, basis, transfer, masked, coeffs, up, v, b, t, c, u, sems):
    move = Mover(sems)
    arrive = [move(vec, v), move(basis, b), move(transfer, t)]
    arrive[0].wait()
    rows = lax.broadcasted_iota(jnp.int32, v.shape, 0)
    v[...] = jnp.where(rows < count_ref[0], v[...].astype(F32), 0.0).astype(BF16)
    leave = [move(v, masked)]
    arrive[1].wait()
    c[...] = dot(b[...], v[...], ((0,), (0,))).astype(BF16)
    leave.append(move(c, coeffs))
    arrive[2].wait()
    u[...] = dot(t[...], c[...], ((0,), (0,))).T.astype(BF16)
    leave.append(move(u, up))
    for copy in leave:
        copy.wait()


def coefficients(count, vec, basis, transfer):
    (rows, vecs), rank = vec.shape, basis.shape[1]
    return call(
        coeff_kernel,
        [count],
        [vec, basis, transfer],
        [shape((rows, vecs)), shape((rank, vecs)), shape((vecs, rank))],
        [
            pltpu.VMEM((rows, vecs), BF16),
            pltpu.VMEM((rows, rank), BF16),
            pltpu.VMEM((rank, rank), BF16),
            pltpu.VMEM((rank, vecs), BF16),
            pltpu.VMEM((vecs, rank), BF16),
        ],
        6,
        cost(2 * rows * rank * vecs, 2 * rows * vecs * 2),
        FULL,
    )


def parent_kernel(pieces, *refs):
    out, terms, total, sems = refs[-4:]
    move = Mover(sems)
    move(pieces, terms).wait()
    total[...] = jnp.sum(terms[...].astype(F32), axis=0).astype(BF16)
    leave = [move(total, out.at[c]) for c in range(X * HALVES)]
    for copy in leave:
        copy.wait()


def parents_of(pieces, before):
    leaves, width, rank = pieces.shape
    return call(
        parent_kernel,
        [],
        [pieces, *before],
        [shape((X * HALVES, width, rank))],
        [pltpu.VMEM(pieces.shape, BF16), pltpu.VMEM((width, rank), BF16)],
        1 + X * HALVES,
        cost(leaves * width * rank, leaves * width * rank * 2),
    )[0]


def top_kernel(mine_ref, coupling, parents_in, *refs):
    out, matrices, parents, value, sems = refs[-5:]
    move = Mover(sems)
    arrive = [move(coupling, matrices), move(parents_in, parents)]
    for copy in arrive:
        copy.wait()
    count = matrices.shape[0]
    value[...] = sum(
        dot(parents[i], matrices[(i + count - 1 - mine_ref[0]) & (count - 1)], ((1,), (1,)))
        for i in range(count)
    ).astype(BF16)
    leave = [move(value, out.at[i]) for i in range(out.shape[0])]
    for copy in leave:
        copy.wait()


def top_field(mine, coupling, parents, copies, before):
    _, width, rank = parents.shape
    return call(
        top_kernel,
        [mine],
        [coupling, parents, *before],
        [shape((copies, width, rank))],
        [
            pltpu.VMEM(coupling.shape, BF16),
            pltpu.VMEM(parents.shape, BF16),
            pltpu.VMEM((width, rank), BF16),
        ],
        copies + 2,
        cost(2 * 8 * width * rank * rank, 8 * rank * rank * 2),
    )[0]


def join_kernel(*refs):
    blocks, out, held, sems = refs[:Z], refs[Z], refs[Z + 1], refs[Z + 2]
    move = Mover(sems)
    arrive = [move(blocks[z], held.at[z]) for z in range(Z)]
    leave = []
    for z in range(Z):
        arrive[z].wait()
        leave.append(move(held.at[z], out.at[z]))
    for copy in leave:
        copy.wait()


def joined(blocks):
    dims = (Z, *blocks[0].shape)
    return call(join_kernel, [], blocks, [shape(dims)], [pltpu.VMEM(dims, BF16)], 2 * Z, cost(0, 0))[0]


def far_kernel(me_ref, far_ref, coupling, *refs):
    stores, (out, matrices, blocks, total, sems) = refs[:ROW], refs[-5:]
    move = Mover(sems)
    me = me_ref[0]
    arrive = move(coupling, matrices)
    copies = []
    for m in range(matrices.shape[0]):
        far = far_ref[m]
        back_z = (me // ROW - far // ROW) & (Z - 1)
        back_y = ((me >> 1) - (far >> 1)) & (Y - 1)
        store = ((far ^ me) & 1) * Y + back_y
        for i, source in enumerate(stores):
            copy = move.later(source.at[back_z], blocks.at[m])
            move.used -= 1
            pl.when(store == i)(copy.start)
        copies.append(move.later(stores[0].at[0], blocks.at[m]))
    arrive.wait()
    for m, copy in enumerate(copies):
        copy.wait()
        value = dot(matrices[m], blocks[m])
        if m:
            total[...] += value
        else:
            total[...] = value
    move(total, out).wait()


def far_field(me, far, coupling, stores, before):
    count, rank, _ = coupling.shape
    vecs = stores[0].shape[2]
    return call(
        far_kernel,
        [me, far],
        [coupling, *stores, *before],
        [shape((rank, vecs), F32)],
        [
            pltpu.VMEM(coupling.shape, BF16),
            pltpu.VMEM((count, rank, vecs), BF16),
            pltpu.VMEM((rank, vecs), F32),
        ],
        count + 2,
        cost(2 * count * rank * rank * vecs, count * rank * vecs * 2),
        FULL,
    )[0]


def tile_for(near_ref, offset):
    found = jnp.int32(-1)
    for k in range(near_ref.shape[0]):
        found = jnp.where(near_ref[k] == offset, jnp.int32(k), found)
    return found


class Products:
    def __init__(self, move, picks, tiles, sources, tile_slots, source_slots):
        self.picks, self.tiles, self.sources = picks, tile_slots, source_slots
        self.copies = []
        for s, pick in enumerate(picks):
            pair = [
                move.later(tiles.at[jnp.maximum(pick, 0)], tile_slots.at[s]),
                move.later(sources[s], source_slots.at[s]),
            ]
            self.copies.append(pair)

            @pl.when(pick >= 0)
            def begin(pair=pair):
                for copy in pair:
                    copy.start()

    def add_to(self, total):
        for s, pick in enumerate(self.picks):

            @pl.when(pick >= 0)
            def add(s=s):
                for copy in self.copies[s]:
                    copy.wait()
                total[...] += dot(self.tiles[s], self.sources[s])


FIRST, LAST = 6, 4


def near_first_kernel(me_ref, near_ref, tiles, *refs):
    sources, (out, tile_slots, source_slots, total, sems) = refs[:FIRST], refs[-5:]
    side = 1 - 2 * (me_ref[0] & 1)
    picks = [tile_for(near_ref, at) for at in (0, side, -2, 2, side - 2, side + 2)]
    move = Mover(sems)
    products = Products(move, picks, tiles, sources, tile_slots, source_slots)
    total[...] = jnp.zeros_like(total)
    products.add_to(total)
    move(total, out).wait()


def near_first(me, near, tiles, sources, before):
    rows, vecs = sources[0].shape
    return call(
        near_first_kernel,
        [me, near],
        [tiles, *sources, *before],
        [shape((rows, vecs), F32)],
        [
            pltpu.VMEM((FIRST, rows, rows), BF16),
            pltpu.VMEM((FIRST, rows, vecs), BF16),
            pltpu.VMEM((rows, vecs), F32),
        ],
        2 * FIRST + 1,
        cost(2 * FIRST * rows * rows * vecs, FIRST * rows * (rows + vecs) * 2),
        FULL,
    )[0]


def near_last_kernel(me_ref, near_ref, count_ref, tiles, *refs):
    sources, refs = refs[:LAST], refs[LAST:]
    near, basis, transfer, far_in, field_in, out = refs[:6]
    tile_slots, source_slots, total, b, t, local, field, sems = refs[6:]
    core = me_ref[0] & 1
    absent = jnp.int32(99)
    places = (-4, 4, jnp.where(core == 0, -3, absent), jnp.where(core == 1, 3, absent))
    picks = [tile_for(near_ref, at) for at in places]
    move = Mover(sems)
    arrive = [move(transfer, t), move(far_in, local), move(field_in, field)]
    arrive += [move(near, total), move(basis, b)]
    products = Products(move, picks, tiles, sources, tile_slots, source_slots)
    for copy in arrive:
        copy.wait()
    local[...] += dot(t[...], field[...], ((1,), (1,)))
    total[...] += dot(b[...], local[...].astype(BF16))
    products.add_to(total)
    live = lax.broadcasted_iota(jnp.int32, total.shape, 0) < count_ref[0]
    total[...] = jnp.where(live, total[...], 0.0)
    move(total, out).wait()


def near_last(me, near_list, count, tiles, sources, near, basis, transfer, far, field):
    (rows, vecs), rank = sources[0].shape, basis.shape[1]
    return call(
        near_last_kernel,
        [me, near_list, count],
        [tiles, *sources, near, basis, transfer, far, field],
        [shape((rows, vecs), F32)],
        [
            pltpu.VMEM((LAST, rows, rows), BF16),
            pltpu.VMEM((LAST, rows, vecs), BF16),
            pltpu.VMEM((rows, vecs), F32),
            pltpu.VMEM((rows, rank), BF16),
            pltpu.VMEM((rank, rank), BF16),
            pltpu.VMEM((rank, vecs), F32),
            pltpu.VMEM((vecs, rank), BF16),
        ],
        2 * LAST + 6,
        cost(2 * LAST * rows * rows * vecs, LAST * rows * (rows + vecs) * 2),
        FULL,
    )[0]


def body(
    vectors,
    near_tiles,
    leaf_basis,
    transfer,
    coupling,
    top_coupling,
    near_list,
    far_list,
    row_counts,
):
    leaf = lax.axis_index("leaf").astype(jnp.int32)
    cluster = lax.axis_index("top").astype(jnp.int32)
    me = leaf[None]
    leaves, clusters = lax.axis_size("leaf"), lax.axis_size("top")
    basis, nested, tiles = leaf_basis[0, 0], transfer[0, 0], near_tiles[0, 0]
    near_offsets, far, count = near_list[0, 0], far_list[0, 0], row_counts[0]
    rank, vecs = nested.shape[0], vectors.shape[3]

    masked, coeffs, up = coefficients(count, vectors[0, 0], basis, nested)

    pieces = exchange("rises", up, None).reshape(leaves, vecs // leaves, rank)
    parent = parents_of(pieces, [])
    parents = exchange("parents", parent, None, "top")

    by_z = [coeffs] + [send(f"coeffs_z{d}", coeffs, turn(d, 0)) for d in range(1, Z)]
    column = joined(after(by_z, pieces))
    stores = [column] + [send(f"coeffs_y{d}", column, turn(0, d)) for d in range(1, Y)]

    beside = send("own_swap", masked, SWAP)
    (masked,) = after([masked], by_z[-1])
    from_low = send("low_hop", masked, chip_step(1))
    from_high = send("high_hop", masked, chip_step(-1))

    field = top_field(cluster[None], top_coupling[0], parents, leaves, [from_low, from_high])
    from_low, from_high = after([from_low, from_high], parents)
    from_low2 = send("low_hop2", from_low, chip_step(1))
    from_high2 = send("high_hop2", from_high, chip_step(-1))
    low_beside = send("low_swap", from_low, SWAP)
    high_beside = send("high_swap", from_high, SWAP)
    near = near_first(
        me,
        near_offsets,
        tiles,
        [masked, beside, from_low, from_high, low_beside, high_beside],
        [field],
    )
    stores += [send(f"coeffs_swap{i}", block, SWAP) for i, block in enumerate(after(stores, parents))]
    field = exchange("fields", field, None).reshape(vecs, rank)
    far_sum = far_field(me, far, coupling[0, 0], stores, [near, field])
    from_low2, from_high2 = after([from_low2, from_high2], far_sum)
    low2_beside = send("low2_swap", from_low2, TO_FIRST)
    high2_beside = send("high2_swap", from_high2, TO_SECOND)
    result = near_last(
        me,
        near_offsets,
        count,
        tiles,
        [from_low2, from_high2, low2_beside, high2_beside],
        near,
        basis,
        nested,
        far_sum,
        field,
    )
    return result[None, None]


def solution(mesh):
    in_specs = (
        P("top", "leaf", None, None),
        P("top", "leaf", None, None, None),
        P("top", "leaf", None, None),
        P("top", "leaf", None, None),
        P("top", "leaf", None, None, None),
        P("top", None, None, None),
        P("top", "leaf", None),
        P("top", "leaf", None),
        P("top", "leaf"),
    )
    out_specs = P("top", "leaf", None, None)
    return jax.shard_map(body, mesh=mesh, in_specs=in_specs, out_specs=out_specs, check_vma=False)
```

```python
import jax
import jax.numpy as jnp
from jax import lax
from jax.experimental import pallas as pl
from jax.experimental.pallas import tpu as pltpu
from jax.sharding import PartitionSpec as P

Z, Y, CORES = 4, 4, 2
ROW = Y * CORES
CHIPS = Z * Y
X, HALVES = 4, 2
F32, BF16 = jnp.float32, jnp.bfloat16
LIMIT, FULL = 40 * 1024 * 1024, 60 * 1024 * 1024


def chip_step(distance):
    return [
        (p * 2 + c, (p + distance) * 2 + c)
        for p in range(CHIPS)
        for c in range(2)
        if 0 <= p + distance < CHIPS
    ]


def seat_of(z, y, c):
    return z * ROW + y * 2 + c


def turn(dz, dy):
    return [
        (seat_of(z, y, c), seat_of((z + dz) % Z, (y + dy) % Y, c))
        for z in range(Z)
        for y in range(Y)
        for c in range(2)
    ]


SWAP = [(i, i ^ 1) for i in range(2 * CHIPS)]
TO_FIRST = [(2 * p + 1, 2 * p) for p in range(CHIPS)]
TO_SECOND = [(2 * p, 2 * p + 1) for p in range(CHIPS)]


def send(name, block, route, axis="leaf"):
    with jax.named_scope(name):
        return lax.ppermute(block, axis, route)


def exchange(name, blocks, groups, axis="leaf"):
    with jax.named_scope(name):
        return lax.all_to_all(blocks, axis, 0, 0, tiled=True, axis_index_groups=groups)


def after(blocks, other):
    return lax.optimization_barrier([*blocks, other])[:-1]


def dot(a, b, dims=((1,), (0,))):
    return lax.dot_general(a, b, (dims, ((), ())), preferred_element_type=F32)


def cost(flops, moved):
    return pl.CostEstimate(flops=int(flops), bytes_accessed=int(moved), transcendentals=0)


ANY = pl.BlockSpec(memory_space=pl.ANY)
SMEM = pl.BlockSpec(memory_space=pltpu.SMEM)


def shape(dims, dtype=BF16):
    return jax.ShapeDtypeStruct(dims, dtype)


def call(kernel, scalars, arrays, outs, scratch, copies, price, limit=LIMIT):
    return pl.pallas_call(
        kernel,
        out_shape=outs,
        in_specs=[SMEM] * len(scalars) + [ANY] * len(arrays),
        out_specs=[ANY] * len(outs),
        scratch_shapes=[*scratch, pltpu.SemaphoreType.DMA((copies,))],
        compiler_params=pltpu.CompilerParams(vmem_limit_bytes=limit),
        cost_estimate=price,
    )(*scalars, *arrays)


class Mover:
    def __init__(self, sems):
        self.sems, self.used = sems, 0

    def __call__(self, src, dst):
        copy = pltpu.make_async_copy(src, dst, self.sems.at[self.used])
        self.used += 1
        copy.start()
        return copy

    def later(self, src, dst):
        copy = pltpu.make_async_copy(src, dst, self.sems.at[self.used])
        self.used += 1
        return copy


def coeff_kernel(count_ref, vec, basis, transfer, masked, coeffs, up, v, b, t, c, u, sems):
    move = Mover(sems)
    arrive = [move(vec, v), move(basis, b), move(transfer, t)]
    arrive[0].wait()
    rows = lax.broadcasted_iota(jnp.int32, v.shape, 0)
    v[...] = jnp.where(rows < count_ref[0], v[...].astype(F32), 0.0).astype(BF16)
    leave = [move(v, masked)]
    arrive[1].wait()
    c[...] = dot(b[...], v[...], ((0,), (0,))).astype(BF16)
    leave.append(move(c, coeffs))
    arrive[2].wait()
    u[...] = dot(t[...], c[...], ((0,), (0,))).T.astype(BF16)
    leave.append(move(u, up))
    for copy in leave:
        copy.wait()


def coefficients(count, vec, basis, transfer):
    (rows, vecs), rank = vec.shape, basis.shape[1]
    return call(
        coeff_kernel,
        [count],
        [vec, basis, transfer],
        [shape((rows, vecs)), shape((rank, vecs)), shape((vecs, rank))],
        [
            pltpu.VMEM((rows, vecs), BF16),
            pltpu.VMEM((rows, rank), BF16),
            pltpu.VMEM((rank, rank), BF16),
            pltpu.VMEM((rank, vecs), BF16),
            pltpu.VMEM((vecs, rank), BF16),
        ],
        6,
        cost(2 * rows * rank * vecs, 2 * rows * vecs * 2),
        FULL,
    )


def parent_kernel(pieces, *refs):
    out, terms, total, sems = refs[-4:]
    move = Mover(sems)
    move(pieces, terms).wait()
    total[...] = jnp.sum(terms[...].astype(F32), axis=0).astype(BF16)
    leave = [move(total, out.at[c]) for c in range(X * HALVES)]
    for copy in leave:
        copy.wait()


def parents_of(pieces, before):
    leaves, width, rank = pieces.shape
    return call(
        parent_kernel,
        [],
        [pieces, *before],
        [shape((X * HALVES, width, rank))],
        [pltpu.VMEM(pieces.shape, BF16), pltpu.VMEM((width, rank), BF16)],
        1 + X * HALVES,
        cost(leaves * width * rank, leaves * width * rank * 2),
    )[0]


def top_kernel(mine_ref, coupling, parents_in, *refs):
    out, matrices, parents, value, sems = refs[-5:]
    move = Mover(sems)
    arrive = [move(coupling, matrices), move(parents_in, parents)]
    for copy in arrive:
        copy.wait()
    count = matrices.shape[0]
    value[...] = sum(
        dot(parents[i], matrices[(i + count - 1 - mine_ref[0]) & (count - 1)], ((1,), (1,)))
        for i in range(count)
    ).astype(BF16)
    leave = [move(value, out.at[i]) for i in range(out.shape[0])]
    for copy in leave:
        copy.wait()


def top_field(mine, coupling, parents, copies, before):
    _, width, rank = parents.shape
    return call(
        top_kernel,
        [mine],
        [coupling, parents, *before],
        [shape((copies, width, rank))],
        [
            pltpu.VMEM(coupling.shape, BF16),
            pltpu.VMEM(parents.shape, BF16),
            pltpu.VMEM((width, rank), BF16),
        ],
        copies + 2,
        cost(2 * 8 * width * rank * rank, 8 * rank * rank * 2),
    )[0]


def join_kernel(*refs):
    blocks, out, held, sems = refs[:Z], refs[Z], refs[Z + 1], refs[Z + 2]
    move = Mover(sems)
    arrive = [move(blocks[z], held.at[z]) for z in range(Z)]
    leave = []
    for z in range(Z):
        arrive[z].wait()
        leave.append(move(held.at[z], out.at[z]))
    for copy in leave:
        copy.wait()


def joined(blocks):
    dims = (Z, *blocks[0].shape)
    return call(join_kernel, [], blocks, [shape(dims)], [pltpu.VMEM(dims, BF16)], 2 * Z, cost(0, 0))[0]


def far_kernel(me_ref, far_ref, coupling, *refs):
    stores, (out, matrices, blocks, total, sems) = refs[:ROW], refs[-5:]
    move = Mover(sems)
    me = me_ref[0]
    arrive = move(coupling, matrices)
    copies = []
    for m in range(matrices.shape[0]):
        far = far_ref[m]
        back_z = (me // ROW - far // ROW) & (Z - 1)
        back_y = ((me >> 1) - (far >> 1)) & (Y - 1)
        store = ((far ^ me) & 1) * Y + back_y
        for i, source in enumerate(stores):
            copy = move.later(source.at[back_z], blocks.at[m])
            move.used -= 1
            pl.when(store == i)(copy.start)
        copies.append(move.later(stores[0].at[0], blocks.at[m]))
    arrive.wait()
    for m, copy in enumerate(copies):
        copy.wait()
        value = dot(matrices[m], blocks[m])
        if m:
            total[...] += value
        else:
            total[...] = value
    move(total, out).wait()


def far_field(me, far, coupling, stores, before):
    count, rank, _ = coupling.shape
    vecs = stores[0].shape[2]
    return call(
        far_kernel,
        [me, far],
        [coupling, *stores, *before],
        [shape((rank, vecs), F32)],
        [
            pltpu.VMEM(coupling.shape, BF16),
            pltpu.VMEM((count, rank, vecs), BF16),
            pltpu.VMEM((rank, vecs), F32),
        ],
        count + 2,
        cost(2 * count * rank * rank * vecs, count * rank * vecs * 2),
        FULL,
    )[0]


def tile_for(near_ref, offset):
    found = jnp.int32(-1)
    for k in range(near_ref.shape[0]):
        found = jnp.where(near_ref[k] == offset, jnp.int32(k), found)
    return found


class Products:
    def __init__(self, move, picks, tiles, sources, tile_slots, source_slots):
        self.picks, self.tiles, self.sources = picks, tile_slots, source_slots
        self.copies = []
        for s, pick in enumerate(picks):
            pair = [
                move.later(tiles.at[jnp.maximum(pick, 0)], tile_slots.at[s]),
                move.later(sources[s], source_slots.at[s]),
            ]
            self.copies.append(pair)

            @pl.when(pick >= 0)
            def begin(pair=pair):
                for copy in pair:
                    copy.start()

    def add_to(self, total):
        for s, pick in enumerate(self.picks):

            @pl.when(pick >= 0)
            def add(s=s):
                for copy in self.copies[s]:
                    copy.wait()
                total[...] += dot(self.tiles[s], self.sources[s])


FIRST, LAST = 6, 4


def near_first_kernel(me_ref, near_ref, tiles, *refs):
    sources, (out, tile_slots, source_slots, total, sems) = refs[:FIRST], refs[-5:]
    side = 1 - 2 * (me_ref[0] & 1)
    picks = [tile_for(near_ref, at) for at in (0, side, -2, 2, side - 2, side + 2)]
    move = Mover(sems)
    products = Products(move, picks, tiles, sources, tile_slots, source_slots)
    total[...] = jnp.zeros_like(total)
    products.add_to(total)
    move(total, out).wait()


def near_first(me, near, tiles, sources, before):
    rows, vecs = sources[0].shape
    return call(
        near_first_kernel,
        [me, near],
        [tiles, *sources, *before],
        [shape((rows, vecs), F32)],
        [
            pltpu.VMEM((FIRST, rows, rows), BF16),
            pltpu.VMEM((FIRST, rows, vecs), BF16),
            pltpu.VMEM((rows, vecs), F32),
        ],
        2 * FIRST + 1,
        cost(2 * FIRST * rows * rows * vecs, FIRST * rows * (rows + vecs) * 2),
        FULL,
    )[0]


def near_last_kernel(me_ref, near_ref, count_ref, tiles, *refs):
    sources, refs = refs[:LAST], refs[LAST:]
    near, basis, transfer, far_in, field_in, out = refs[:6]
    tile_slots, source_slots, total, b, t, local, field, sems = refs[6:]
    core = me_ref[0] & 1
    absent = jnp.int32(99)
    places = (-4, 4, jnp.where(core == 0, -3, absent), jnp.where(core == 1, 3, absent))
    picks = [tile_for(near_ref, at) for at in places]
    move = Mover(sems)
    arrive = [move(transfer, t), move(far_in, local), move(field_in, field)]
    arrive += [move(near, total), move(basis, b)]
    products = Products(move, picks, tiles, sources, tile_slots, source_slots)
    for copy in arrive:
        copy.wait()
    local[...] += dot(t[...], field[...], ((1,), (1,)))
    total[...] += dot(b[...], local[...].astype(BF16))
    products.add_to(total)
    live = lax.broadcasted_iota(jnp.int32, total.shape, 0) < count_ref[0]
    total[...] = jnp.where(live, total[...], 0.0)
    move(total, out).wait()


def near_last(me, near_list, count, tiles, sources, near, basis, transfer, far, field):
    (rows, vecs), rank = sources[0].shape, basis.shape[1]
    return call(
        near_last_kernel,
        [me, near_list, count],
        [tiles, *sources, near, basis, transfer, far, field],
        [shape((rows, vecs), F32)],
        [
            pltpu.VMEM((LAST, rows, rows), BF16),
            pltpu.VMEM((LAST, rows, vecs), BF16),
            pltpu.VMEM((rows, vecs), F32),
            pltpu.VMEM((rows, rank), BF16),
            pltpu.VMEM((rank, rank), BF16),
            pltpu.VMEM((rank, vecs), F32),
            pltpu.VMEM((vecs, rank), BF16),
        ],
        2 * LAST + 6,
        cost(2 * LAST * rows * rows * vecs, LAST * rows * (rows + vecs) * 2),
        FULL,
    )[0]


def body(
    vectors,
    near_tiles,
    leaf_basis,
    transfer,
    coupling,
    top_coupling,
    near_list,
    far_list,
    row_counts,
):
    leaf = lax.axis_index("leaf").astype(jnp.int32)
    cluster = lax.axis_index("top").astype(jnp.int32)
    me = leaf[None]
    leaves, clusters = lax.axis_size("leaf"), lax.axis_size("top")
    basis, nested, tiles = leaf_basis[0, 0], transfer[0, 0], near_tiles[0, 0]
    near_offsets, far, count = near_list[0, 0], far_list[0, 0], row_counts[0]
    rank, vecs = nested.shape[0], vectors.shape[3]

    masked, coeffs, up = coefficients(count, vectors[0, 0], basis, nested)

    pieces = exchange("rises", up, None).reshape(leaves, vecs // leaves, rank)
    parent = parents_of(pieces, [])
    parents = exchange("parents", parent, None, "top")

    by_z = [coeffs] + [send(f"coeffs_z{d}", coeffs, turn(d, 0)) for d in range(1, Z)]
    column = joined(after(by_z, pieces))
    stores = [column] + [send(f"coeffs_y{d}", column, turn(0, d)) for d in range(1, Y)]

    beside = send("own_swap", masked, SWAP)
    from_low = send("low_hop", masked, chip_step(1))
    from_high = send("high_hop", masked, chip_step(-1))

    field = top_field(cluster[None], top_coupling[0], parents, leaves, [from_low, from_high])
    from_low, from_high = after([from_low, from_high], parents)
    from_low2 = send("low_hop2", from_low, chip_step(1))
    from_high2 = send("high_hop2", from_high, chip_step(-1))
    low_beside = send("low_swap", from_low, SWAP)
    high_beside = send("high_swap", from_high, SWAP)
    near = near_first(
        me,
        near_offsets,
        tiles,
        [masked, beside, from_low, from_high, low_beside, high_beside],
        [field],
    )
    stores += [send(f"coeffs_swap{i}", block, SWAP) for i, block in enumerate(after(stores, parents))]
    field = exchange("fields", field, None).reshape(vecs, rank)
    far_sum = far_field(me, far, coupling[0, 0], stores, [near])
    from_low2, from_high2 = after(after([from_low2, from_high2], far_sum), field)
    low2_beside = send("low2_swap", from_low2, TO_FIRST)
    high2_beside = send("high2_swap", from_high2, TO_SECOND)
    result = near_last(
        me,
        near_offsets,
        count,
        tiles,
        [from_low2, from_high2, low2_beside, high2_beside],
        near,
        basis,
        nested,
        far_sum,
        field,
    )
    return result[None, None]


def solution(mesh):
    in_specs = (
        P("top", "leaf", None, None),
        P("top", "leaf", None, None, None),
        P("top", "leaf", None, None),
        P("top", "leaf", None, None),
        P("top", "leaf", None, None, None),
        P("top", None, None, None),
        P("top", "leaf", None),
        P("top", "leaf", None),
        P("top", "leaf"),
    )
    out_specs = P("top", "leaf", None, None)
    return jax.shard_map(body, mesh=mesh, in_specs=in_specs, out_specs=out_specs, check_vma=False)
```

```python
import jax
import jax.numpy as jnp
from jax import lax
from jax.experimental import pallas as pl
from jax.experimental.pallas import tpu as pltpu
from jax.sharding import PartitionSpec as P

Z, Y, CORES = 4, 4, 2
ROW = Y * CORES
CHIPS = Z * Y
X, HALVES = 4, 2
F32, BF16 = jnp.float32, jnp.bfloat16
LIMIT, FULL = 40 * 1024 * 1024, 60 * 1024 * 1024


def chip_step(distance):
    return [
        (p * 2 + c, (p + distance) * 2 + c)
        for p in range(CHIPS)
        for c in range(2)
        if 0 <= p + distance < CHIPS
    ]


def seat_of(z, y, c):
    return z * ROW + y * 2 + c


def turn(dz, dy):
    return [
        (seat_of(z, y, c), seat_of((z + dz) % Z, (y + dy) % Y, c))
        for z in range(Z)
        for y in range(Y)
        for c in range(2)
    ]


SWAP = [(i, i ^ 1) for i in range(2 * CHIPS)]
TO_FIRST = [(2 * p + 1, 2 * p) for p in range(CHIPS)]
TO_SECOND = [(2 * p, 2 * p + 1) for p in range(CHIPS)]


def send(name, block, route, axis="leaf"):
    with jax.named_scope(name):
        return lax.ppermute(block, axis, route)


def exchange(name, blocks, groups, axis="leaf"):
    with jax.named_scope(name):
        return lax.all_to_all(blocks, axis, 0, 0, tiled=True, axis_index_groups=groups)


def after(blocks, other):
    return lax.optimization_barrier([*blocks, other])[:-1]


def dot(a, b, dims=((1,), (0,))):
    return lax.dot_general(a, b, (dims, ((), ())), preferred_element_type=F32)


def cost(flops, moved):
    return pl.CostEstimate(flops=int(flops), bytes_accessed=int(moved), transcendentals=0)


ANY = pl.BlockSpec(memory_space=pl.ANY)
SMEM = pl.BlockSpec(memory_space=pltpu.SMEM)


def shape(dims, dtype=BF16):
    return jax.ShapeDtypeStruct(dims, dtype)


def call(kernel, scalars, arrays, outs, scratch, copies, price, limit=LIMIT):
    return pl.pallas_call(
        kernel,
        out_shape=outs,
        in_specs=[SMEM] * len(scalars) + [ANY] * len(arrays),
        out_specs=[ANY] * len(outs),
        scratch_shapes=[*scratch, pltpu.SemaphoreType.DMA((copies,))],
        compiler_params=pltpu.CompilerParams(vmem_limit_bytes=limit),
        cost_estimate=price,
    )(*scalars, *arrays)


class Mover:
    def __init__(self, sems):
        self.sems, self.used = sems, 0

    def __call__(self, src, dst):
        copy = pltpu.make_async_copy(src, dst, self.sems.at[self.used])
        self.used += 1
        copy.start()
        return copy

    def later(self, src, dst):
        copy = pltpu.make_async_copy(src, dst, self.sems.at[self.used])
        self.used += 1
        return copy


def coeff_kernel(count_ref, vec, basis, transfer, masked, coeffs, up, v, b, t, c, u, sems):
    move = Mover(sems)
    arrive = [move(vec, v), move(basis, b), move(transfer, t)]
    arrive[0].wait()
    rows = lax.broadcasted_iota(jnp.int32, v.shape, 0)
    v[...] = jnp.where(rows < count_ref[0], v[...].astype(F32), 0.0).astype(BF16)
    leave = [move(v, masked)]
    arrive[1].wait()
    c[...] = dot(b[...], v[...], ((0,), (0,))).astype(BF16)
    leave.append(move(c, coeffs))
    arrive[2].wait()
    u[...] = dot(t[...], c[...], ((0,), (0,))).T.astype(BF16)
    leave.append(move(u, up))
    for copy in leave:
        copy.wait()


def coefficients(count, vec, basis, transfer):
    (rows, vecs), rank = vec.shape, basis.shape[1]
    return call(
        coeff_kernel,
        [count],
        [vec, basis, transfer],
        [shape((rows, vecs)), shape((rank, vecs)), shape((vecs, rank))],
        [
            pltpu.VMEM((rows, vecs), BF16),
            pltpu.VMEM((rows, rank), BF16),
            pltpu.VMEM((rank, rank), BF16),
            pltpu.VMEM((rank, vecs), BF16),
            pltpu.VMEM((vecs, rank), BF16),
        ],
        6,
        cost(2 * rows * rank * vecs, 2 * rows * vecs * 2),
        FULL,
    )


def parent_kernel(pieces, *refs):
    out, terms, total, sems = refs[-4:]
    move = Mover(sems)
    move(pieces, terms).wait()
    total[...] = jnp.sum(terms[...].astype(F32), axis=0).astype(BF16)
    leave = [move(total, out.at[c]) for c in range(X * HALVES)]
    for copy in leave:
        copy.wait()


def parents_of(pieces, before):
    leaves, width, rank = pieces.shape
    return call(
        parent_kernel,
        [],
        [pieces, *before],
        [shape((X * HALVES, width, rank))],
        [pltpu.VMEM(pieces.shape, BF16), pltpu.VMEM((width, rank), BF16)],
        1 + X * HALVES,
        cost(leaves * width * rank, leaves * width * rank * 2),
    )[0]


def top_kernel(mine_ref, coupling, parents_in, *refs):
    out, matrices, parents, value, sems = refs[-5:]
    move = Mover(sems)
    arrive = [move(coupling, matrices), move(parents_in, parents)]
    for copy in arrive:
        copy.wait()
    count = matrices.shape[0]
    value[...] = sum(
        dot(parents[i], matrices[(i + count - 1 - mine_ref[0]) & (count - 1)], ((1,), (1,)))
        for i in range(count)
    ).astype(BF16)
    leave = [move(value, out.at[i]) for i in range(out.shape[0])]
    for copy in leave:
        copy.wait()


def top_field(mine, coupling, parents, copies, before):
    _, width, rank = parents.shape
    return call(
        top_kernel,
        [mine],
        [coupling, parents, *before],
        [shape((copies, width, rank))],
        [
            pltpu.VMEM(coupling.shape, BF16),
            pltpu.VMEM(parents.shape, BF16),
            pltpu.VMEM((width, rank), BF16),
        ],
        copies + 2,
        cost(2 * 8 * width * rank * rank, 8 * rank * rank * 2),
    )[0]


def join_kernel(*refs):
    blocks, out, held, sems = refs[:Z], refs[Z], refs[Z + 1], refs[Z + 2]
    move = Mover(sems)
    arrive = [move(blocks[z], held.at[z]) for z in range(Z)]
    leave = []
    for z in range(Z):
        arrive[z].wait()
        leave.append(move(held.at[z], out.at[z]))
    for copy in leave:
        copy.wait()


def joined(blocks):
    dims = (Z, *blocks[0].shape)
    return call(join_kernel, [], blocks, [shape(dims)], [pltpu.VMEM(dims, BF16)], 2 * Z, cost(0, 0))[0]


def far_kernel(me_ref, far_ref, coupling, *refs):
    stores, (out, matrices, blocks, total, sems) = refs[:ROW], refs[-5:]
    move = Mover(sems)
    me = me_ref[0]
    arrive = move(coupling, matrices)
    copies = []
    for m in range(matrices.shape[0]):
        far = far_ref[m]
        back_z = (me // ROW - far // ROW) & (Z - 1)
        back_y = ((me >> 1) - (far >> 1)) & (Y - 1)
        store = ((far ^ me) & 1) * Y + back_y
        for i, source in enumerate(stores):
            copy = move.later(source.at[back_z], blocks.at[m])
            move.used -= 1
            pl.when(store == i)(copy.start)
        copies.append(move.later(stores[0].at[0], blocks.at[m]))
    arrive.wait()
    for m, copy in enumerate(copies):
        copy.wait()
        value = dot(matrices[m], blocks[m])
        if m:
            total[...] += value
        else:
            total[...] = value
    move(total, out).wait()


def far_field(me, far, coupling, stores, before):
    count, rank, _ = coupling.shape
    vecs = stores[0].shape[2]
    return call(
        far_kernel,
        [me, far],
        [coupling, *stores, *before],
        [shape((rank, vecs), F32)],
        [
            pltpu.VMEM(coupling.shape, BF16),
            pltpu.VMEM((count, rank, vecs), BF16),
            pltpu.VMEM((rank, vecs), F32),
        ],
        count + 2,
        cost(2 * count * rank * rank * vecs, count * rank * vecs * 2),
        FULL,
    )[0]


def tile_for(near_ref, offset):
    found = jnp.int32(-1)
    for k in range(near_ref.shape[0]):
        found = jnp.where(near_ref[k] == offset, jnp.int32(k), found)
    return found


class Products:
    def __init__(self, move, picks, tiles, sources, tile_slots, source_slots):
        self.picks, self.tiles, self.sources = picks, tile_slots, source_slots
        self.copies = []
        for s, pick in enumerate(picks):
            pair = [
                move.later(tiles.at[jnp.maximum(pick, 0)], tile_slots.at[s]),
                move.later(sources[s], source_slots.at[s]),
            ]
            self.copies.append(pair)

            @pl.when(pick >= 0)
            def begin(pair=pair):
                for copy in pair:
                    copy.start()

    def add_to(self, total):
        for s, pick in enumerate(self.picks):

            @pl.when(pick >= 0)
            def add(s=s):
                for copy in self.copies[s]:
                    copy.wait()
                total[...] += dot(self.tiles[s], self.sources[s])


FIRST, LAST = 6, 2


def near_first_kernel(me_ref, near_ref, tiles, *refs):
    sources, (out, tile_slots, source_slots, total, sems) = refs[:FIRST], refs[-5:]
    side = 1 - 2 * (me_ref[0] & 1)
    picks = [tile_for(near_ref, at) for at in (0, side, -2, 2, side - 2, side + 2)]
    move = Mover(sems)
    products = Products(move, picks, tiles, sources, tile_slots, source_slots)
    total[...] = jnp.zeros_like(total)
    products.add_to(total)
    move(total, out).wait()


def near_first(me, near, tiles, sources, before):
    rows, vecs = sources[0].shape
    return call(
        near_first_kernel,
        [me, near],
        [tiles, *sources, *before],
        [shape((rows, vecs), F32)],
        [
            pltpu.VMEM((FIRST, rows, rows), BF16),
            pltpu.VMEM((FIRST, rows, vecs), BF16),
            pltpu.VMEM((rows, vecs), F32),
        ],
        2 * FIRST + 1,
        cost(2 * FIRST * rows * rows * vecs, FIRST * rows * (rows + vecs) * 2),
        FULL,
    )[0]


def near_second_kernel(near_ref, tiles, *refs):
    sources, refs = refs[:LAST], refs[LAST:]
    near, basis, transfer, far_in, field_in, out = refs[:6]
    tile_slots, source_slots, total, b, t, local, field, sems = refs[6:]
    picks = [tile_for(near_ref, at) for at in (-4, 4)]
    move = Mover(sems)
    arrive = [move(transfer, t), move(far_in, local), move(field_in, field)]
    arrive += [move(near, total), move(basis, b)]
    products = Products(move, picks, tiles, sources, tile_slots, source_slots)
    for copy in arrive:
        copy.wait()
    local[...] += dot(t[...], field[...], ((1,), (1,)))
    total[...] += dot(b[...], local[...].astype(BF16))
    products.add_to(total)
    move(total, out).wait()


def near_second(near_list, tiles, sources, near, basis, transfer, far, field):
    (rows, vecs), rank = sources[0].shape, basis.shape[1]
    return call(
        near_second_kernel,
        [near_list],
        [tiles, *sources, near, basis, transfer, far, field],
        [shape((rows, vecs), F32)],
        [
            pltpu.VMEM((LAST, rows, rows), BF16),
            pltpu.VMEM((LAST, rows, vecs), BF16),
            pltpu.VMEM((rows, vecs), F32),
            pltpu.VMEM((rows, rank), BF16),
            pltpu.VMEM((rank, rank), BF16),
            pltpu.VMEM((rank, vecs), F32),
            pltpu.VMEM((vecs, rank), BF16),
        ],
        2 * LAST + 6,
        cost(2 * LAST * rows * rows * vecs, LAST * rows * (rows + vecs) * 2),
        FULL,
    )[0]


def near_last_kernel(me_ref, near_ref, count_ref, tiles, *refs):
    sources, (near, out, tile_slots, source_slots, total, sems) = refs[:LAST], refs[LAST:]
    core = me_ref[0] & 1
    absent = jnp.int32(99)
    places = (jnp.where(core == 0, -3, absent), jnp.where(core == 1, 3, absent))
    picks = [tile_for(near_ref, at) for at in places]
    move = Mover(sems)
    arrive = move(near, total)
    products = Products(move, picks, tiles, sources, tile_slots, source_slots)
    arrive.wait()
    products.add_to(total)
    live = lax.broadcasted_iota(jnp.int32, total.shape, 0) < count_ref[0]
    total[...] = jnp.where(live, total[...], 0.0)
    move(total, out).wait()


def near_last(me, near_list, count, tiles, sources, near):
    rows, vecs = sources[0].shape
    return call(
        near_last_kernel,
        [me, near_list, count],
        [tiles, *sources, near],
        [shape((rows, vecs), F32)],
        [
            pltpu.VMEM((LAST, rows, rows), BF16),
            pltpu.VMEM((LAST, rows, vecs), BF16),
            pltpu.VMEM((rows, vecs), F32),
        ],
        2 * LAST + 2,
        cost(2 * LAST * rows * rows * vecs, LAST * rows * (rows + vecs) * 2),
        FULL,
    )[0]


def body(
    vectors,
    near_tiles,
    leaf_basis,
    transfer,
    coupling,
    top_coupling,
    near_list,
    far_list,
    row_counts,
):
    leaf = lax.axis_index("leaf").astype(jnp.int32)
    cluster = lax.axis_index("top").astype(jnp.int32)
    me = leaf[None]
    leaves, clusters = lax.axis_size("leaf"), lax.axis_size("top")
    basis, nested, tiles = leaf_basis[0, 0], transfer[0, 0], near_tiles[0, 0]
    near_offsets, far, count = near_list[0, 0], far_list[0, 0], row_counts[0]
    rank, vecs = nested.shape[0], vectors.shape[3]

    masked, coeffs, up = coefficients(count, vectors[0, 0], basis, nested)

    pieces = exchange("rises", up, None).reshape(leaves, vecs // leaves, rank)
    parent = parents_of(pieces, [])
    parents = exchange("parents", parent, None, "top")

    by_z = [coeffs] + [send(f"coeffs_z{d}", coeffs, turn(d, 0)) for d in range(1, Z)]
    column = joined(after(by_z, pieces))
    stores = [column] + [send(f"coeffs_y{d}", column, turn(0, d)) for d in range(1, Y)]

    beside = send("own_swap", masked, SWAP)
    from_low = send("low_hop", masked, chip_step(1))
    from_high = send("high_hop", masked, chip_step(-1))

    field = top_field(cluster[None], top_coupling[0], parents, leaves, [from_low, from_high])
    from_low, from_high = after([from_low, from_high], parents)
    from_low2 = send("low_hop2", from_low, chip_step(1))
    from_high2 = send("high_hop2", from_high, chip_step(-1))
    low_beside = send("low_swap", from_low, SWAP)
    high_beside = send("high_swap", from_high, SWAP)
    near = near_first(
        me,
        near_offsets,
        tiles,
        [masked, beside, from_low, from_high, low_beside, high_beside],
        [field],
    )
    stores += [send(f"coeffs_swap{i}", block, SWAP) for i, block in enumerate(after(stores, parents))]
    field = exchange("fields", field, None).reshape(vecs, rank)
    far_sum = far_field(me, far, coupling[0, 0], stores, [near])
    from_low2, from_high2 = after(after([from_low2, from_high2], far_sum), field)
    low2_beside = send("low2_swap", from_low2, TO_FIRST)
    high2_beside = send("high2_swap", from_high2, TO_SECOND)
    near = near_second(
        near_offsets,
        tiles,
        [from_low2, from_high2],
        near,
        basis,
        nested,
        far_sum,
        field,
    )
    result = near_last(me, near_offsets, count, tiles, [low2_beside, high2_beside], near)
    return result[None, None]


def solution(mesh):
    in_specs = (
        P("top", "leaf", None, None),
        P("top", "leaf", None, None, None),
        P("top", "leaf", None, None),
        P("top", "leaf", None, None),
        P("top", "leaf", None, None, None),
        P("top", None, None, None),
        P("top", "leaf", None),
        P("top", "leaf", None),
        P("top", "leaf"),
    )
    out_specs = P("top", "leaf", None, None)
    return jax.shard_map(body, mesh=mesh, in_specs=in_specs, out_specs=out_specs, check_vma=False)
```

```python
import jax
import jax.numpy as jnp
from jax import lax
from jax.experimental import pallas as pl
from jax.experimental.pallas import tpu as pltpu
from jax.sharding import PartitionSpec as P

Z, Y, CORES = 4, 4, 2
ROW = Y * CORES
CHIPS = Z * Y
X, HALVES = 4, 2
F32, BF16 = jnp.float32, jnp.bfloat16
LIMIT, FULL = 40 * 1024 * 1024, 60 * 1024 * 1024


def chip_step(distance):
    return [
        (p * 2 + c, (p + distance) * 2 + c)
        for p in range(CHIPS)
        for c in range(2)
        if 0 <= p + distance < CHIPS
    ]


def seat_of(z, y, c):
    return z * ROW + y * 2 + c


def turn(dz, dy):
    return [
        (seat_of(z, y, c), seat_of((z + dz) % Z, (y + dy) % Y, c))
        for z in range(Z)
        for y in range(Y)
        for c in range(2)
    ]


SWAP = [(i, i ^ 1) for i in range(2 * CHIPS)]


def send(name, block, route, axis="leaf"):
    with jax.named_scope(name):
        return lax.ppermute(block, axis, route)


def exchange(name, blocks, groups, axis="leaf"):
    with jax.named_scope(name):
        return lax.all_to_all(blocks, axis, 0, 0, tiled=True, axis_index_groups=groups)


def after(blocks, other):
    return lax.optimization_barrier([*blocks, other])[:-1]


def dot(a, b, dims=((1,), (0,))):
    return lax.dot_general(a, b, (dims, ((), ())), preferred_element_type=F32)


def cost(flops, moved):
    return pl.CostEstimate(flops=int(flops), bytes_accessed=int(moved), transcendentals=0)


ANY = pl.BlockSpec(memory_space=pl.ANY)
SMEM = pl.BlockSpec(memory_space=pltpu.SMEM)


def shape(dims, dtype=BF16):
    return jax.ShapeDtypeStruct(dims, dtype)


def call(kernel, scalars, arrays, outs, scratch, copies, price, limit=LIMIT):
    return pl.pallas_call(
        kernel,
        out_shape=outs,
        in_specs=[SMEM] * len(scalars) + [ANY] * len(arrays),
        out_specs=[ANY] * len(outs),
        scratch_shapes=[*scratch, pltpu.SemaphoreType.DMA((copies,))],
        compiler_params=pltpu.CompilerParams(vmem_limit_bytes=limit),
        cost_estimate=price,
    )(*scalars, *arrays)


class Mover:
    def __init__(self, sems):
        self.sems, self.used = sems, 0

    def __call__(self, src, dst):
        copy = pltpu.make_async_copy(src, dst, self.sems.at[self.used])
        self.used += 1
        copy.start()
        return copy

    def later(self, src, dst):
        copy = pltpu.make_async_copy(src, dst, self.sems.at[self.used])
        self.used += 1
        return copy


def coeff_kernel(count_ref, vec, basis, transfer, masked, coeffs, up, v, b, t, c, u, sems):
    move = Mover(sems)
    arrive = [move(vec, v), move(basis, b), move(transfer, t)]
    arrive[0].wait()
    rows = lax.broadcasted_iota(jnp.int32, v.shape, 0)
    v[...] = jnp.where(rows < count_ref[0], v[...].astype(F32), 0.0).astype(BF16)
    leave = [move(v, masked)]
    arrive[1].wait()
    c[...] = dot(b[...], v[...], ((0,), (0,))).astype(BF16)
    leave.append(move(c, coeffs))
    arrive[2].wait()
    u[...] = dot(t[...], c[...], ((0,), (0,))).T.astype(BF16)
    leave.append(move(u, up))
    for copy in leave:
        copy.wait()


def coefficients(count, vec, basis, transfer):
    (rows, vecs), rank = vec.shape, basis.shape[1]
    return call(
        coeff_kernel,
        [count],
        [vec, basis, transfer],
        [shape((rows, vecs)), shape((rank, vecs)), shape((vecs, rank))],
        [
            pltpu.VMEM((rows, vecs), BF16),
            pltpu.VMEM((rows, rank), BF16),
            pltpu.VMEM((rank, rank), BF16),
            pltpu.VMEM((rank, vecs), BF16),
            pltpu.VMEM((vecs, rank), BF16),
        ],
        6,
        cost(2 * rows * rank * vecs, 2 * rows * vecs * 2),
        FULL,
    )


def parent_kernel(pieces, *refs):
    out, terms, total, sems = refs[-4:]
    move = Mover(sems)
    move(pieces, terms).wait()
    total[...] = jnp.sum(terms[...].astype(F32), axis=0).astype(BF16)
    leave = [move(total, out.at[c]) for c in range(X * HALVES)]
    for copy in leave:
        copy.wait()


def parents_of(pieces, before):
    leaves, width, rank = pieces.shape
    return call(
        parent_kernel,
        [],
        [pieces, *before],
        [shape((X * HALVES, width, rank))],
        [pltpu.VMEM(pieces.shape, BF16), pltpu.VMEM((width, rank), BF16)],
        1 + X * HALVES,
        cost(leaves * width * rank, leaves * width * rank * 2),
    )[0]


def top_kernel(mine_ref, coupling, parents_in, *refs):
    out, matrices, parents, value, sems = refs[-5:]
    move = Mover(sems)
    arrive = [move(coupling, matrices), move(parents_in, parents)]
    for copy in arrive:
        copy.wait()
    count = matrices.shape[0]
    value[...] = sum(
        dot(parents[i], matrices[(i + count - 1 - mine_ref[0]) & (count - 1)], ((1,), (1,)))
        for i in range(count)
    ).astype(BF16)
    leave = [move(value, out.at[i]) for i in range(out.shape[0])]
    for copy in leave:
        copy.wait()


def top_field(mine, coupling, parents, copies, before):
    _, width, rank = parents.shape
    return call(
        top_kernel,
        [mine],
        [coupling, parents, *before],
        [shape((copies, width, rank))],
        [
            pltpu.VMEM(coupling.shape, BF16),
            pltpu.VMEM(parents.shape, BF16),
            pltpu.VMEM((width, rank), BF16),
        ],
        copies + 2,
        cost(2 * 8 * width * rank * rank, 8 * rank * rank * 2),
    )[0]


def join_kernel(*refs):
    blocks, out, held, sems = refs[:Z], refs[Z], refs[Z + 1], refs[Z + 2]
    move = Mover(sems)
    arrive = [move(blocks[z], held.at[z]) for z in range(Z)]
    leave = []
    for z in range(Z):
        arrive[z].wait()
        leave.append(move(held.at[z], out.at[z]))
    for copy in leave:
        copy.wait()


def joined(blocks):
    dims = (Z, *blocks[0].shape)
    return call(join_kernel, [], blocks, [shape(dims)], [pltpu.VMEM(dims, BF16)], 2 * Z, cost(0, 0))[0]


def far_kernel(me_ref, far_ref, coupling, *refs):
    stores, (out, matrices, blocks, total, sems) = refs[:ROW], refs[-5:]
    move = Mover(sems)
    me = me_ref[0]
    arrive = move(coupling, matrices)
    copies = []
    for m in range(matrices.shape[0]):
        far = far_ref[m]
        back_z = (me // ROW - far // ROW) & (Z - 1)
        back_y = ((me >> 1) - (far >> 1)) & (Y - 1)
        store = ((far ^ me) & 1) * Y + back_y
        for i, source in enumerate(stores):
            copy = move.later(source.at[back_z], blocks.at[m])
            move.used -= 1
            pl.when(store == i)(copy.start)
        copies.append(move.later(stores[0].at[0], blocks.at[m]))
    arrive.wait()
    for m, copy in enumerate(copies):
        copy.wait()
        value = dot(matrices[m], blocks[m])
        if m:
            total[...] += value
        else:
            total[...] = value
    move(total, out).wait()


def far_field(me, far, coupling, stores, before):
    count, rank, _ = coupling.shape
    vecs = stores[0].shape[2]
    return call(
        far_kernel,
        [me, far],
        [coupling, *stores, *before],
        [shape((rank, vecs), F32)],
        [
            pltpu.VMEM(coupling.shape, BF16),
            pltpu.VMEM((count, rank, vecs), BF16),
            pltpu.VMEM((rank, vecs), F32),
        ],
        count + 2,
        cost(2 * count * rank * rank * vecs, count * rank * vecs * 2),
        FULL,
    )[0]


def tile_for(near_ref, offset):
    found = jnp.int32(-1)
    for k in range(near_ref.shape[0]):
        found = jnp.where(near_ref[k] == offset, jnp.int32(k), found)
    return found


class Products:
    def __init__(self, move, picks, tiles, sources, tile_slots, source_slots):
        self.picks, self.tiles, self.sources = picks, tile_slots, source_slots
        self.copies = []
        for s, pick in enumerate(picks):
            pair = [
                move.later(tiles.at[jnp.maximum(pick, 0)], tile_slots.at[s]),
                move.later(sources[s], source_slots.at[s]),
            ]
            self.copies.append(pair)

            @pl.when(pick >= 0)
            def begin(pair=pair):
                for copy in pair:
                    copy.start()

    def add_to(self, total):
        for s, pick in enumerate(self.picks):

            @pl.when(pick >= 0)
            def add(s=s):
                for copy in self.copies[s]:
                    copy.wait()
                total[...] += dot(self.tiles[s], self.sources[s])


FIRST, LAST = 6, 3


def near_first_kernel(me_ref, near_ref, tiles, *refs):
    sources, (out, tile_slots, source_slots, total, sems) = refs[:FIRST], refs[-5:]
    side = 1 - 2 * (me_ref[0] & 1)
    picks = [tile_for(near_ref, at) for at in (0, side, -2, 2, side - 2, side + 2)]
    move = Mover(sems)
    products = Products(move, picks, tiles, sources, tile_slots, source_slots)
    total[...] = jnp.zeros_like(total)
    products.add_to(total)
    move(total, out).wait()


def near_first(me, near, tiles, sources, before):
    rows, vecs = sources[0].shape
    return call(
        near_first_kernel,
        [me, near],
        [tiles, *sources, *before],
        [shape((rows, vecs), F32)],
        [
            pltpu.VMEM((FIRST, rows, rows), BF16),
            pltpu.VMEM((FIRST, rows, vecs), BF16),
            pltpu.VMEM((rows, vecs), F32),
        ],
        2 * FIRST + 1,
        cost(2 * FIRST * rows * rows * vecs, FIRST * rows * (rows + vecs) * 2),
        FULL,
    )[0]


def near_last_kernel(me_ref, near_ref, count_ref, tiles, *refs):
    sources, refs = refs[:LAST], refs[LAST:]
    near, basis, transfer, far_in, field_in, out = refs[:6]
    tile_slots, source_slots, total, b, t, local, field, sems = refs[6:]
    places = (-4, 4, jnp.where((me_ref[0] & 1) == 0, -3, 3))
    picks = [tile_for(near_ref, at) for at in places]
    move = Mover(sems)
    arrive = [move(transfer, t), move(far_in, local), move(field_in, field)]
    arrive += [move(near, total), move(basis, b)]
    products = Products(move, picks, tiles, sources, tile_slots, source_slots)
    for copy in arrive:
        copy.wait()
    local[...] += dot(t[...], field[...], ((1,), (1,)))
    total[...] += dot(b[...], local[...].astype(BF16))
    products.add_to(total)
    live = lax.broadcasted_iota(jnp.int32, total.shape, 0) < count_ref[0]
    total[...] = jnp.where(live, total[...], 0.0)
    move(total, out).wait()


def near_last(me, near_list, count, tiles, sources, near, basis, transfer, far, field):
    (rows, vecs), rank = sources[0].shape, basis.shape[1]
    return call(
        near_last_kernel,
        [me, near_list, count],
        [tiles, *sources, near, basis, transfer, far, field],
        [shape((rows, vecs), F32)],
        [
            pltpu.VMEM((LAST, rows, rows), BF16),
            pltpu.VMEM((LAST, rows, vecs), BF16),
            pltpu.VMEM((rows, vecs), F32),
            pltpu.VMEM((rows, rank), BF16),
            pltpu.VMEM((rank, rank), BF16),
            pltpu.VMEM((rank, vecs), F32),
            pltpu.VMEM((vecs, rank), BF16),
        ],
        2 * LAST + 6,
        cost(2 * LAST * rows * rows * vecs, LAST * rows * (rows + vecs) * 2),
        FULL,
    )[0]


def body(
    vectors,
    near_tiles,
    leaf_basis,
    transfer,
    coupling,
    top_coupling,
    near_list,
    far_list,
    row_counts,
):
    leaf = lax.axis_index("leaf").astype(jnp.int32)
    cluster = lax.axis_index("top").astype(jnp.int32)
    me = leaf[None]
    leaves, clusters = lax.axis_size("leaf"), lax.axis_size("top")
    basis, nested, tiles = leaf_basis[0, 0], transfer[0, 0], near_tiles[0, 0]
    near_offsets, far, count = near_list[0, 0], far_list[0, 0], row_counts[0]
    rank, vecs = nested.shape[0], vectors.shape[3]

    masked, coeffs, up = coefficients(count, vectors[0, 0], basis, nested)

    pieces = exchange("rises", up, None).reshape(leaves, vecs // leaves, rank)
    parent = parents_of(pieces, [])
    parents = exchange("parents", parent, None, "top")

    by_z = [coeffs] + [send(f"coeffs_z{d}", coeffs, turn(d, 0)) for d in range(1, Z)]
    column = joined(after(by_z, pieces))
    stores = [column] + [send(f"coeffs_y{d}", column, turn(0, d)) for d in range(1, Y)]

    beside = send("own_swap", masked, SWAP)
    from_low = send("low_hop", masked, chip_step(1))
    from_high = send("high_hop", masked, chip_step(-1))

    field = top_field(cluster[None], top_coupling[0], parents, leaves, [from_low, from_high])
    from_low, from_high = after([from_low, from_high], parents)
    from_low2 = send("low_hop2", from_low, chip_step(1))
    from_high2 = send("high_hop2", from_high, chip_step(-1))
    low_beside = send("low_swap", from_low, SWAP)
    high_beside = send("high_swap", from_high, SWAP)
    near = near_first(
        me,
        near_offsets,
        tiles,
        [masked, beside, from_low, from_high, low_beside, high_beside],
        [field],
    )
    stores += [send(f"coeffs_swap{i}", block, SWAP) for i, block in enumerate(after(stores, parents))]
    field = exchange("fields", field, None).reshape(vecs, rank)
    far_sum = far_field(me, far, coupling[0, 0], stores, [near])
    from_low2, from_high2 = after(after([from_low2, from_high2], far_sum), field)
    wanted = jnp.where(leaf % 2 == 0, from_high2, from_low2)
    beside2 = send("second_swap", wanted, SWAP)
    result = near_last(
        me,
        near_offsets,
        count,
        tiles,
        [from_low2, from_high2, beside2],
        near,
        basis,
        nested,
        far_sum,
        field,
    )
    return result[None, None]


def solution(mesh):
    in_specs = (
        P("top", "leaf", None, None),
        P("top", "leaf", None, None, None),
        P("top", "leaf", None, None),
        P("top", "leaf", None, None),
        P("top", "leaf", None, None, None),
        P("top", None, None, None),
        P("top", "leaf", None),
        P("top", "leaf", None),
        P("top", "leaf"),
    )
    out_specs = P("top", "leaf", None, None)
    return jax.shard_map(body, mesh=mesh, in_specs=in_specs, out_specs=out_specs, check_vma=False)
```
